256 devices in a mesh: leaf: 16 (over z_hi, y, core), row: 4 (over z_lo), col: 4 (over x).
Axes of the slice: x: 4, y: 4, z: 8 (z_hi: 2, z_lo: 4; z = z_hi * 4 + z_lo), core: 2. Of those that a mesh axis runs over, the one named last changes fastest.
Arguments:
- root_inverse: bfloat16 [2, 1536, 1536], P(None, 'row', 'col'), may hold values from -4 to 4
- parent_link: bfloat16 [2, 1536, 6144], P(None, 'row', ('leaf', 'col')), may hold values from -0.15625 to 0.15625
- parent_pivot: bfloat16 [2, 1536, 6144], P(None, 'row', ('leaf', 'col')), may hold values from -4 to 4
- child_link_parent: bfloat16 [2, 16, 1536, 1536], P(None, 'leaf', 'row', 'col'), may hold values from -0.15625 to 0.15625
- child_link_root: bfloat16 [2, 16, 1536, 1536], P(None, 'leaf', 'row', 'col'), may hold values from -0.15625 to 0.15625
- child_pivot: bfloat16 [2, 16, 1536, 1536], P(None, 'leaf', 'row', 'col'), may hold values from -4 to 4
- link_pattern: int32 [16, 2, 12, 12], P('leaf', None, 'row', 'col'), may hold values 0 or 1
Outputs:
- root_parent_inv: bfloat16 [2, 1536, 6144], P(None, 'row', ('leaf', 'col'))
- parent_inv: bfloat16 [2, 1536, 6144], P(None, 'row', ('leaf', 'col'))
- child_parent_inv: bfloat16 [2, 16, 1536, 1536], P(None, 'leaf', 'row', 'col')
- child_root_inv: bfloat16 [2, 16, 1536, 1536], P(None, 'leaf', 'row', 'col')
- child_inv: bfloat16 [2, 16, 1536, 1536], P(None, 'leaf', 'row', 'col')
The draws below stay inside these ranges and needn't reach their ends.
All inputs are finite; a program needn't handle non-finite values. No bound on the sum of `link_pattern` on one device may be relied on, other than what follows from the above.
Results may differ from the reference program's by a relative error of at most 0.02.
Values may be sent and summed in bfloat16 or wider, within the bound.
No kernel may reach another device: no remote copies, remote signals or barrier semaphores. Data moves between devices by JAX's collectives and lax.ppermute only.
A program may use at most 64 MiB of HBM per device.

```python
import jax
import jax.numpy as jnp
from jax import lax

SN = 1536
BLK = 128
POLES = 2
NP = 4
N_LEAF = 16
N_ROW = 4


def with_ends(array, stream_key, low, high):
    spot = [jax.random.randint(jax.random.fold_in(stream_key, axis), (), 0, length) for axis, length in enumerate(array.shape)]
    widest = array.shape.index(max(array.shape))
    neighbour = spot[:widest] + [(spot[widest] + 1) % array.shape[widest]] + spot[widest + 1:]
    return array.at[tuple(spot)].set(low).at[tuple(neighbour)].set(high)


def level_of(own_key, dims, pieces, low, high):
    factor_of, own = 1.0, jax.random.fold_in(own_key, 6)
    for axis_at, parts in pieces:
        draws = jnp.exp(jax.random.uniform(jax.random.fold_in(own, axis_at), (parts,), jnp.float32, low / len(pieces), high / len(pieces)))
        factor_of = factor_of * jnp.repeat(draws, dims[axis_at] // parts).reshape([-1 if axis == axis_at else 1 for axis in range(len(dims))])
    return factor_of


def normal_values(stream_key, dims, spread, reach, split=(), held_as=jnp.bfloat16):
    entries = spread * jax.random.normal(stream_key, dims, jnp.float32)
    if split:
        entries = entries * level_of(stream_key, dims, split, -0.22, 0.18)
    return jnp.clip(entries, -reach, reach).astype(held_as)


def setup_inputs(seed: int = 0) -> dict:
    streams_of = jax.random.split(jax.random.key(seed), 8)
    return {
        "root_inverse": normal_values(streams_of[0], (POLES, SN, SN), 0.5, 4.0, ((1, 4), (2, 4))),
        "parent_link": normal_values(streams_of[1], (POLES, SN, NP * SN), SN ** -0.5, 0.15625, ((1, 4), (2, 64))),
        "parent_pivot": normal_values(streams_of[2], (POLES, SN, NP * SN), 0.5, 4.0, ((1, 4), (2, 64))),
        "child_link_parent": normal_values(streams_of[3], (POLES, N_LEAF, SN, SN), SN ** -0.5, 0.15625, ((1, 16), (2, 4), (3, 4))),
        "child_link_root": normal_values(streams_of[4], (POLES, N_LEAF, SN, SN), SN ** -0.5, 0.15625, ((1, 16), (2, 4), (3, 4))),
        "child_pivot": normal_values(streams_of[5], (POLES, N_LEAF, SN, SN), 0.5, 4.0, ((1, 16), (2, 4), (3, 4))),
        "link_pattern": with_ends((jax.random.randint(streams_of[6], (N_LEAF, 2, SN // BLK, SN // BLK), 0, 4) < 3).astype(jnp.int32), jax.random.fold_in(streams_of[6], 1), 0, 1),
    }


def product(left, right):
    return jnp.dot(left, right, preferred_element_type=jnp.float32)


def rounded(value):
    return lax.optimization_barrier(value.astype(jnp.bfloat16)).astype(jnp.float32)


def sliced(pairs):
    slice_rows = pairs[0][0].shape[0] // N_ROW
    total = None
    for slice_index in range(N_ROW):
        lower = slice_index * slice_rows
        upper = lower + slice_rows
        term = None
        for left, right in pairs:
            piece = product(left[lower:upper].T, right[lower:upper])
            term = piece if term is None else term + piece
        term = rounded(term)
        total = term if total is None else total + term
    return total


def expand(pattern):
    return jnp.repeat(jnp.repeat(pattern, BLK, axis=0), BLK, axis=1).astype(jnp.bfloat16)


def reference(root_inverse, parent_link, parent_pivot, child_link_parent, child_link_root, child_pivot, link_pattern):
    fan_out = min(4, N_LEAF)
    outs_rp, outs_pp, outs_ps, outs_rs, outs_ss = [], [], [], [], []
    for pole_index in range(POLES):
        root_block = root_inverse[pole_index]
        rp_list, pp_list = [], []
        for parent_index in range(N_LEAF // fan_out):
            link = parent_link[pole_index][:, parent_index * SN:(parent_index + 1) * SN]
            pivot = parent_pivot[pole_index][:, parent_index * SN:(parent_index + 1) * SN]
            root_parent = (-product(root_block, link)).astype(jnp.bfloat16)
            parent_self = (pivot.astype(jnp.float32) - sliced([(link, root_parent)])).astype(jnp.bfloat16)
            rp_list.append(root_parent)
            pp_list.append(parent_self)
        ps_list, rs_list, ss_list = [], [], []
        for child_index in range(N_LEAF):
            parent_index = child_index // fan_out
            root_parent = rp_list[parent_index]
            parent_self = pp_list[parent_index]
            link_parent = child_link_parent[pole_index, child_index] * expand(link_pattern[child_index, 0])
            link_root = child_link_root[pole_index, child_index] * expand(link_pattern[child_index, 1])
            child_parent = (-(product(parent_self, link_parent) + sliced([(root_parent, link_root)]))).astype(jnp.bfloat16)
            child_root = (-(product(root_parent, link_parent) + product(root_block, link_root))).astype(jnp.bfloat16)
            child_self = (child_pivot[pole_index, child_index].astype(jnp.float32)
                          - sliced([(link_parent, child_parent), (link_root, child_root)])).astype(jnp.bfloat16)
            ps_list.append(child_parent)
            rs_list.append(child_root)
            ss_list.append(child_self)
        outs_rp.append(jnp.concatenate(rp_list, axis=1))
        outs_pp.append(jnp.concatenate(pp_list, axis=1))
        outs_ps.append(jnp.stack(ps_list))
        outs_rs.append(jnp.stack(rs_list))
        outs_ss.append(jnp.stack(ss_list))
    return (jnp.stack(outs_rp), jnp.stack(outs_pp), jnp.stack(outs_ps), jnp.stack(outs_rs), jnp.stack(outs_ss))
```

```python
import jax
import jax.numpy as jnp
from jax import lax
from jax.sharding import PartitionSpec as P

BF16 = jnp.bfloat16
F32 = jnp.float32


def exchange(block, axis, bits):
    count = lax.axis_size(axis)
    return lax.ppermute(block, axis, [(i, i ^ bits) for i in range(count)])


def in_order(pieces, index):
    odd = (index & 1) == 1
    high = (index & 2) == 2
    a, b, c, d = pieces
    a, b = jnp.where(odd, b, a), jnp.where(odd, a, b)
    c, d = jnp.where(odd, d, c), jnp.where(odd, c, d)
    return [
        jnp.where(high, c, a),
        jnp.where(high, d, b),
        jnp.where(high, a, c),
        jnp.where(high, b, d),
    ]


def fetched(block, axis):
    one = exchange(block, axis, 1)
    three = exchange(block, axis, 3)
    two = exchange(block, axis, 2)
    return [block, one, two, three]


def pick(array, index):
    return lax.dynamic_index_in_dim(array, index, 0, keepdims=False)


def pair(flag, first, second):
    return jnp.where(flag, jnp.concatenate([second, first]), jnp.concatenate([first, second]))


def dot(left, right, dims):
    return lax.dot_general(left, right, (dims, ((), ())), preferred_element_type=F32)


def all_rows(block, row):
    lower = row < 2
    near = pair((row & 1) == 1, block[None], exchange(block, "row", 1)[None])
    middle = lax.ppermute(near, "row", [(1, 2), (2, 1)])
    outer = lax.ppermute(middle, "row", [(1, 0), (2, 3)])
    far = jnp.where((row == 1) | (row == 2), middle, outer)
    return pair(~lower, near, far)


def expand(pattern, size):
    return jnp.repeat(jnp.repeat(pattern, size, axis=1), size, axis=2).astype(BF16)


def shards(
    root_inverse,
    parent_link,
    parent_pivot,
    child_link_parent,
    child_link_root,
    child_pivot,
    link_pattern,
):
    leaf, row, col = (lax.axis_index(name) for name in ("leaf", "row", "col"))
    core = leaf & 1
    odd_core = core == 1
    odd_chip = (leaf & 2) == 2
    b = root_inverse.shape[-1]
    w = parent_link.shape[-1]

    def kept(array):
        return pick(array, core)

    def given(array):
        return pick(array, 1 - core)

    small = jnp.stack([parent_link, parent_pivot], 1).swapaxes(2, 3)
    small_here, small_there = kept(small), exchange(given(small), "leaf", 1)
    link_two = pair(odd_core, small_here[0], small_there[0])
    pivot_two = pair(odd_core, small_here[1], small_there[1])
    factors = jnp.stack([child_link_parent[:, 0], child_link_root[:, 0]], 1)
    factors = factors * expand(link_pattern[0], b // link_pattern.shape[2])[None]
    own, guest = kept(factors), exchange(given(factors), "leaf", 1)
    pivots = child_pivot[:, 0]
    own_pivot, guest_pivot = kept(pivots), exchange(given(pivots), "leaf", 1)
    root = kept(root_inverse)

    across = fetched(jnp.concatenate([root, link_two]), "col")
    root_rows = jnp.concatenate(in_order([p[:b] for p in across], col), 1)
    down = jnp.concatenate(in_order(fetched(link_two, "row"), row), 1)
    root_parent = (-dot(down, root_rows, ((1,), (1,)))).astype(BF16)

    links = jnp.stack(in_order([p[b:].reshape(2, w, b) for p in across], col), 1)
    links = pair(odd_chip, links, exchange(links, "leaf", 2)).reshape(4, 4 * w, b)
    guest_rows = lax.all_gather(guest, "col")
    own_rows = lax.all_gather(own, "col")
    parts = [dot(root_parent, pick(links, row ^ d), ((1,), (1,))).astype(BF16) for d in range(4)]
    total = parts[0].astype(F32)
    for d in (1, 3, 2):
        total = total + exchange(parts[d], "row", d).astype(F32)
    parent_self = (pivot_two.astype(F32) - total).astype(BF16)

    four = pair(odd_chip, root_parent, exchange(root_parent, "leaf", 2)).reshape(4, w, b)
    turned = [pick(four, row)] + [exchange(pick(four, row ^ d), "row", d) for d in (1, 2, 3)]
    turned = jnp.stack(in_order(turned, row))
    across = fetched(jnp.concatenate([four, turned]), "col")
    cross = jnp.stack(in_order([p[:4] for p in across], col), 1).reshape(16 * w, b)
    turned = jnp.stack(in_order([p[4:] for p in across], col))
    turned = turned.transpose(0, 2, 1, 3).reshape(4 * w, 4 * b)
    four = pair(odd_chip, parent_self, exchange(parent_self, "leaf", 2)).reshape(4, w, b)
    parents = jnp.stack(in_order(fetched(four, "col"), col), 1).reshape(16 * w, b)

    def child(block, rows, pivot):
        whole = all_rows(block, row)
        upper, lower = whole[:, 0].reshape(4 * b, b), whole[:, 1].reshape(4 * b, b)
        child_parent = -(dot(parents, upper, ((0,), (0,))) + dot(turned, lower, ((1,), (0,))))
        child_root = -(dot(cross, upper, ((0,), (0,))) + dot(root_rows, lower, ((1,), (0,))))
        child_parent, child_root = child_parent.astype(BF16), child_root.astype(BF16)
        terms = []
        for d in range(4):
            mine = pick(rows, row ^ d)
            term = dot(mine[0], child_parent, ((0,), (0,))) + dot(mine[1], child_root, ((0,), (0,)))
            terms.append(term.astype(BF16))
        total = terms[0].astype(F32)
        for d in (1, 3, 2):
            total = total + exchange(terms[d], "row", d).astype(F32)
        return jnp.stack([child_parent, child_root]), (pivot.astype(F32) - total).astype(BF16)

    guest_pair, guest_self = child(guest, guest_rows, guest_pivot)
    guest_pair, guest_self = exchange(guest_pair, "leaf", 1), exchange(guest_self, "leaf", 1)
    own_pair, own_self = child(own, own_rows, own_pivot)

    both = jnp.stack([root_parent, parent_self]).reshape(2, 2, w, b)
    both_there = exchange(jnp.where(odd_core, both[:, 0], both[:, 1]), "leaf", 1)
    both_here = jnp.where(odd_core, both[:, 1], both[:, 0])
    both = pair(odd_core, both_here[None], both_there[None]).swapaxes(2, 3)
    pairs = pair(odd_core, own_pair[None], guest_pair[None])
    selfs = pair(odd_core, own_self[None], guest_self[None])
    return (both[:, 0], both[:, 1], pairs[:, 0][:, None], pairs[:, 1][:, None], selfs[:, None])


def solution(mesh):
    in_specs = (
        P(None, "row", "col"),
        P(None, "row", ("leaf", "col")),
        P(None, "row", ("leaf", "col")),
        P(None, "leaf", "row", "col"),
        P(None, "leaf", "row", "col"),
        P(None, "leaf", "row", "col"),
        P("leaf", None, "row", "col"),
    )
    out_specs = (
        P(None, "row", ("leaf", "col")),
        P(None, "row", ("leaf", "col")),
        P(None, "leaf", "row", "col"),
        P(None, "leaf", "row", "col"),
        P(None, "leaf", "row", "col"),
    )
    return jax.shard_map(shards, mesh=mesh, in_specs=in_specs, out_specs=out_specs, check_vma=False)
```

```python
import jax
import jax.numpy as jnp
from jax import lax
from jax.sharding import PartitionSpec as P

BF16 = jnp.bfloat16
F32 = jnp.float32


def exchange(block, axis, bits):
    count = lax.axis_size(axis)
    return lax.ppermute(block, axis, [(i, i ^ bits) for i in range(count)])


def in_order(pieces, index):
    odd = (index & 1) == 1
    high = (index & 2) == 2
    a, b, c, d = pieces
    a, b = jnp.where(odd, b, a), jnp.where(odd, a, b)
    c, d = jnp.where(odd, d, c), jnp.where(odd, c, d)
    return [
        jnp.where(high, c, a),
        jnp.where(high, d, b),
        jnp.where(high, a, c),
        jnp.where(high, b, d),
    ]


def fetched(block, axis):
    half = block.shape[0] // 2
    one, three = exchange(block, axis, 1), exchange(block, axis, 3)
    two = jnp.concatenate([exchange(one[:half], axis, 3), exchange(three[half:], axis, 1)])
    return [block, one, two, three]


def pick(array, index):
    return lax.dynamic_index_in_dim(array, index, 0, keepdims=False)


def pair(flag, first, second):
    return jnp.where(flag, jnp.concatenate([second, first]), jnp.concatenate([first, second]))


def dot(left, right, dims):
    return lax.dot_general(left, right, (dims, ((), ())), preferred_element_type=F32)


def doubled(block, row, first=None):
    far = pair(row >= 2, block[None], (exchange(block, "row", 2) if first is None else first)[None])
    near = exchange(far, "row", 1)
    odd = (row & 1) == 1
    both = jnp.where(odd, jnp.stack([near, far], 1), jnp.stack([far, near], 1))
    return both.reshape(4, *block.shape)


def halved(term, row):
    side, high = row & 1, row >> 1
    sent = jnp.stack([term(1 - side).astype(BF16), term(3 - side).astype(BF16)])
    came = exchange(sent, "row", 1).astype(F32)
    low_sum, high_sum = term(side) + came[0], term(side + 2) + came[1]
    passed = jnp.where(high == 1, low_sum, high_sum).astype(BF16)
    return jnp.where(high == 1, high_sum, low_sum) + exchange(passed, "row", 2).astype(F32)


def turned_rows(four, row):
    side, high = row & 1, row >> 1
    halves = four.reshape(2, 2, *four.shape[1:])
    mine, came = pick(halves, high), exchange(pick(halves, 1 - high), "row", 2)
    far = pair(high == 1, mine[None], came[None])
    kept = lax.dynamic_index_in_dim(far, side, 1, keepdims=False)
    near = exchange(lax.dynamic_index_in_dim(far, 1 - side, 1, keepdims=False), "row", 1)
    both = jnp.where(side == 1, jnp.stack([near, kept], 1), jnp.stack([kept, near], 1))
    return both.reshape(4, *four.shape[1:])


def expand(pattern, size):
    return jnp.repeat(jnp.repeat(pattern, size, axis=1), size, axis=2).astype(BF16)


def shards(
    root_inverse,
    parent_link,
    parent_pivot,
    child_link_parent,
    child_link_root,
    child_pivot,
    link_pattern,
):
    leaf, row, col = (lax.axis_index(name) for name in ("leaf", "row", "col"))
    core = leaf & 1
    odd_core = core == 1
    odd_chip = (leaf & 2) == 2
    b = root_inverse.shape[-1]
    w = parent_link.shape[-1]

    def kept(array):
        return pick(array, core)

    def given(array):
        return pick(array, 1 - core)

    small = jnp.stack([parent_link, parent_pivot], 1).swapaxes(2, 3)
    small_here, small_there = kept(small), exchange(given(small), "leaf", 1)
    link_two = pair(odd_core, small_here[0], small_there[0])
    pivot_two = pair(odd_core, small_here[1], small_there[1])
    factors = jnp.stack([child_link_parent[:, 0], child_link_root[:, 0]], 1)
    factors = factors * expand(link_pattern[0], b // link_pattern.shape[2])[None]
    own, guest = kept(factors), exchange(given(factors), "leaf", 1)
    pivots = child_pivot[:, 0]
    own_pivot, guest_pivot = kept(pivots), exchange(given(pivots), "leaf", 1)
    root = kept(root_inverse)

    root_rows = jnp.concatenate(in_order(fetched(root, "col"), col), 1)
    links = pair(odd_chip, link_two, exchange(link_two, "leaf", 2)).reshape(4, w, b)
    links = lax.all_gather(links, "col")
    down = doubled(link_two, row).swapaxes(0, 1).reshape(2 * w, 4 * b)
    root_parent = (-dot(down, root_rows, ((1,), (1,)))).astype(BF16)
    guest_first = exchange(guest, "row", 2)
    late_own, _ = lax.optimization_barrier((own, guest_first))
    own_first = exchange(late_own, "row", 2)

    late_guest, links = lax.optimization_barrier((guest, links))
    guest_rows = lax.all_gather(late_guest, "col")
    late_own, guest_rows = lax.optimization_barrier((own, guest_rows))
    own_rows = lax.all_gather(late_own, "col")

    def parent_term(m):
        block = lax.dynamic_index_in_dim(links, m, 1, keepdims=False).reshape(4 * w, b)
        return dot(root_parent, block, ((1,), (1,)))

    parent_self = (pivot_two.astype(F32) - halved(parent_term, row)).astype(BF16)

    four = pair(odd_chip, root_parent, exchange(root_parent, "leaf", 2)).reshape(4, w, b)
    across = fetched(jnp.concatenate([four, turned_rows(four, row)]), "col")
    cross = jnp.stack(in_order([p[:4] for p in across], col), 1).reshape(16 * w, b)
    turned = jnp.stack(in_order([p[4:] for p in across], col))
    turned = turned.transpose(0, 2, 1, 3).reshape(4 * w, 4 * b)
    four = pair(odd_chip, parent_self, exchange(parent_self, "leaf", 2)).reshape(4, w, b)
    parents = jnp.stack(in_order(fetched(four, "col"), col), 1).reshape(16 * w, b)
    by_parent = jnp.concatenate([parents, cross], 1)
    by_root = jnp.concatenate([turned, root_rows])

    def child(block, first, rows, pivot):
        whole = doubled(block, row, first)
        upper, lower = whole[:, 0].reshape(4 * b, b), whole[:, 1].reshape(4 * b, b)
        down = -(dot(by_parent, upper, ((0,), (0,))) + dot(by_root, lower, ((1,), (0,))))
        down = down.astype(BF16)

        def term(m):
            return dot(pick(rows, m).reshape(2 * b, b), down, ((0,), (0,)))

        return down, (pivot.astype(F32) - halved(term, row)).astype(BF16)

    guest_pair, guest_self = child(guest, guest_first, guest_rows, guest_pivot)
    guest_pair, guest_self = exchange(guest_pair, "leaf", 1), exchange(guest_self, "leaf", 1)
    own_pair, own_self = child(own, own_first, own_rows, own_pivot)

    both = jnp.stack([root_parent, parent_self]).reshape(2, 2, w, b)
    both_there = exchange(jnp.where(odd_core, both[:, 0], both[:, 1]), "leaf", 1)
    both_here = jnp.where(odd_core, both[:, 1], both[:, 0])
    both = pair(odd_core, both_here[None], both_there[None]).swapaxes(2, 3)
    pairs = pair(odd_core, own_pair[None], guest_pair[None])
    selfs = pair(odd_core, own_self[None], guest_self[None])
    pairs = pairs.reshape(2, 2, 1, b, b)
    return (both[:, 0], both[:, 1], pairs[:, 0], pairs[:, 1], selfs[:, None])


def solution(mesh):
    in_specs = (
        P(None, "row", "col"),
        P(None, "row", ("leaf", "col")),
        P(None, "row", ("leaf", "col")),
        P(None, "leaf", "row", "col"),
        P(None, "leaf", "row", "col"),
        P(None, "leaf", "row", "col"),
        P("leaf", None, "row", "col"),
    )
    out_specs = (
        P(None, "row", ("leaf", "col")),
        P(None, "row", ("leaf", "col")),
        P(None, "leaf", "row", "col"),
        P(None, "leaf", "row", "col"),
        P(None, "leaf", "row", "col"),
    )
    return jax.shard_map(shards, mesh=mesh, in_specs=in_specs, out_specs=out_specs, check_vma=False)
```

```python
import jax
import jax.numpy as jnp
from jax import lax
from jax.sharding import PartitionSpec as P

BF16 = jnp.bfloat16
F32 = jnp.float32


def exchange(block, axis, bits):
    count = lax.axis_size(axis)
    return lax.ppermute(block, axis, [(i, i ^ bits) for i in range(count)])


def in_order(pieces, index):
    odd = (index & 1) == 1
    high = (index & 2) == 2
    a, b, c, d = pieces
    a, b = jnp.where(odd, b, a), jnp.where(odd, a, b)
    c, d = jnp.where(odd, d, c), jnp.where(odd, c, d)
    return [
        jnp.where(high, c, a),
        jnp.where(high, d, b),
        jnp.where(high, a, c),
        jnp.where(high, b, d),
    ]


def ring_first(block, axis):
    return exchange(block, axis, 1), exchange(block, axis, 3)


def ring_second(one, three):
    half = one.shape[0] // 2
    return three[half:], one[:half]


def fetched(block, axis):
    one, three = exchange(block, axis, 1), exchange(block, axis, 3)
    return [block, one, exchange(block, axis, 2), three]


def after(*arrays):
    total = jnp.int32(0)
    for array in arrays:
        value = array[(0,) * array.ndim].astype(F32)
        total = total + jnp.minimum(jnp.abs(jnp.clip(value, -1, 1).astype(jnp.int32)), 0)
    return total


def ring_rest(block, one, three):
    left, right = ring_second(one, three)
    opposite = jnp.concatenate([exchange(right, "col", 3), exchange(left, "col", 1)])
    return [block, one, opposite, three]


def pick(array, index):
    return lax.dynamic_index_in_dim(array, index, 0, keepdims=False)


def pair(flag, first, second):
    return jnp.where(flag, jnp.concatenate([second, first]), jnp.concatenate([first, second]))


def dot(left, right, dims):
    return lax.dot_general(left, right, (dims, ((), ())), preferred_element_type=F32)


def halved(term, row):
    side, high = row & 1, row >> 1
    sent = jnp.stack([term(1 - side).astype(BF16), term(3 - side).astype(BF16)])
    came = exchange(sent, "row", 1).astype(F32)
    low_sum, high_sum = term(side) + came[0], term(side + 2) + came[1]
    passed = jnp.where(high == 1, low_sum, high_sum).astype(BF16)
    return jnp.where(high == 1, high_sum, low_sum) + exchange(passed, "row", 2).astype(F32)


def turned_rows(four, row):
    side, high = row & 1, row >> 1
    halves = four.reshape(2, 2, *four.shape[1:])
    mine, came = pick(halves, high), exchange(pick(halves, 1 - high), "row", 2)
    far = pair(high == 1, mine[None], came[None])
    kept = lax.dynamic_index_in_dim(far, side, 1, keepdims=False)
    near = exchange(lax.dynamic_index_in_dim(far, 1 - side, 1, keepdims=False), "row", 1)
    both = jnp.where(side == 1, jnp.stack([near, kept], 1), jnp.stack([kept, near], 1))
    return both.reshape(4, *four.shape[1:])


def expand(pattern, size):
    return jnp.repeat(jnp.repeat(pattern, size, axis=1), size, axis=2).astype(BF16)


def shards(
    root_inverse,
    parent_link,
    parent_pivot,
    child_link_parent,
    child_link_root,
    child_pivot,
    link_pattern,
):
    leaf, row, col = (lax.axis_index(name) for name in ("leaf", "row", "col"))
    core = leaf & 1
    odd_core = core == 1
    odd_chip = (leaf & 2) == 2
    b = root_inverse.shape[-1]
    w = parent_link.shape[-1]

    def kept(array, late=0):
        return pick(array, core + late)

    def given(array, late=0):
        return pick(array, 1 - core + late)

    factors = jnp.stack([child_link_parent[:, 0], child_link_root[:, 0]], 1)
    factors = factors * expand(link_pattern[0], b // link_pattern.shape[2])[None]
    own = kept(factors)
    own_whole = lax.all_gather(own, "row")
    guest = exchange(given(factors), "leaf", 1)
    root = kept(root_inverse)
    root_one, root_three = ring_first(root, "col")

    small = jnp.stack([parent_link, parent_pivot], 1).swapaxes(2, 3)
    small_here, small_gift = kept(small), given(small)
    small_there = exchange(small_gift, "leaf", 1)
    link_two = pair(odd_core, small_here[0], small_there[0])
    link_far = pair(
        odd_core, exchange(small_here[0], "leaf", 2), exchange(small_gift[0], "leaf", 3)
    )
    link_four = pair(odd_chip, link_two, link_far)

    column = in_order(fetched(small[:, 0], "row"), row)
    column = jnp.concatenate(column, 2)
    down = pair(odd_core, kept(column), exchange(given(column), "leaf", 1))
    left, right = ring_second(root_one, root_three)
    came_one = exchange(jnp.concatenate([left, link_four]), "col", 1)
    came_three = exchange(jnp.concatenate([right, link_four]), "col", 3)
    half = b // 2
    root_two = jnp.concatenate([came_three[:half], came_one[:half]])
    root_rows = jnp.concatenate(in_order([root, root_one, root_two, root_three], col), 1)
    root_parent = (-dot(down, root_rows, ((1,), (1,)))).astype(BF16)
    links = ring_rest(link_four, came_one[half:], came_three[half:])
    far_off = row + after(links[2]) < 0
    bulk = jnp.where(far_off, jnp.stack([guest, own]), jnp.stack([own, guest]))
    bulk_one, bulk_three = ring_first(bulk, "col")
    links = [p.reshape(4, w, b) for p in links]
    links = jnp.stack(in_order(links, col), 1).reshape(4, 4 * w, b)
    late = after(own_whole)
    total = halved(lambda m: dot(root_parent, pick(links, m + late), ((1,), (1,))), row)
    pivot_two = pair(core + after(bulk_one, bulk_three) == 1, small_here[1], small_there[1])
    parent_self = (pivot_two.astype(F32) - total).astype(BF16)
    pivots = child_pivot[:, 0]
    own_pivot, guest_pivot = kept(pivots), exchange(given(pivots), "leaf", 1)

    cross = pair(odd_chip, root_parent, exchange(root_parent, "leaf", 2)).reshape(4, w, b)
    turned = turned_rows(cross, row)
    guest_whole = lax.all_gather(guest, "row")
    parents = pair(odd_chip, parent_self, exchange(parent_self, "leaf", 2)).reshape(4, w, b)
    across = jnp.concatenate([cross, turned, parents])
    across_one, across_three = ring_first(across, "col")
    across = ring_rest(across, across_one, across_three)
    bulk = ring_rest(bulk, bulk_one, bulk_three)
    cross = jnp.stack(in_order([p[:4] for p in across], col), 1).reshape(16 * w, b)
    turned = jnp.stack(in_order([p[4:8] for p in across], col))
    turned = turned.transpose(0, 2, 1, 3).reshape(4 * w, 4 * b)
    parents = jnp.stack(in_order([p[8:] for p in across], col), 1).reshape(16 * w, b)

    def child(whole, rows, pivot, late):
        upper = lax.dynamic_index_in_dim(whole, late, 1).reshape(4 * b, b)
        lower = lax.dynamic_index_in_dim(whole, 1 + late, 1).reshape(4 * b, b)
        child_parent = -(dot(parents, upper, ((0,), (0,))) + dot(turned, lower, ((1,), (0,))))
        child_root = -(dot(cross, upper, ((0,), (0,))) + dot(root_rows, lower, ((1,), (0,))))
        child_parent, child_root = child_parent.astype(BF16), child_root.astype(BF16)

        def term(m):
            mine = pick(rows, m)
            return dot(mine[0], child_parent, ((0,), (0,))) + dot(mine[1], child_root, ((0,), (0,)))

        total = halved(term, row)
        return jnp.stack([child_parent, child_root]), (pivot.astype(F32) - total).astype(BF16)

    rows = [jnp.stack(in_order([p[i] for p in bulk], col)) for i in range(2)]
    own_pair, own_self = child(own_whole, rows[0], own_pivot, 0)
    guest_pair, guest_self = child(guest_whole, rows[1], guest_pivot, after(own_pair))
    guest_pair, guest_self = exchange(guest_pair, "leaf", 1), exchange(guest_self, "leaf", 1)

    both = jnp.stack([root_parent, parent_self]).reshape(2, 2, w, b)
    both_there = exchange(jnp.where(odd_core, both[:, 0], both[:, 1]), "leaf", 1)
    both_here = jnp.where(odd_core, both[:, 1], both[:, 0])
    both = pair(odd_core, both_here[None], both_there[None]).swapaxes(2, 3)
    pairs = pair(odd_core, own_pair[None], guest_pair[None])
    selfs = pair(odd_core, own_self[None], guest_self[None])
    return (both[:, 0], both[:, 1], pairs[:, 0][:, None], pairs[:, 1][:, None], selfs[:, None])


def solution(mesh):
    in_specs = (
        P(None, "row", "col"),
        P(None, "row", ("leaf", "col")),
        P(None, "row", ("leaf", "col")),
        P(None, "leaf", "row", "col"),
        P(None, "leaf", "row", "col"),
        P(None, "leaf", "row", "col"),
        P("leaf", None, "row", "col"),
    )
    out_specs = (
        P(None, "row", ("leaf", "col")),
        P(None, "row", ("leaf", "col")),
        P(None, "leaf", "row", "col"),
        P(None, "leaf", "row", "col"),
        P(None, "leaf", "row", "col"),
    )
    return jax.shard_map(shards, mesh=mesh, in_specs=in_specs, out_specs=out_specs, check_vma=False)
```

```python
import jax
import jax.numpy as jnp
from jax import lax
from jax.sharding import PartitionSpec as P

BF16 = jnp.bfloat16
F32 = jnp.float32


def exchange(block, axis, bits):
    count = lax.axis_size(axis)
    return lax.ppermute(block, axis, [(i, i ^ bits) for i in range(count)])


def in_order(pieces, index):
    odd = (index & 1) == 1
    high = (index & 2) == 2
    a, b, c, d = pieces
    a, b = jnp.where(odd, b, a), jnp.where(odd, a, b)
    c, d = jnp.where(odd, d, c), jnp.where(odd, c, d)
    return [
        jnp.where(high, c, a),
        jnp.where(high, d, b),
        jnp.where(high, a, c),
        jnp.where(high, b, d),
    ]


def ring_first(block, axis):
    return exchange(block, axis, 1), exchange(block, axis, 3)


def ring_second(one, three):
    half = one.shape[0] // 2
    return three[half:], one[:half]


def fetched(block, axis):
    one, three = exchange(block, axis, 1), exchange(block, axis, 3)
    return [block, one, exchange(block, axis, 2), three]


def after(*arrays):
    total = jnp.int32(0)
    for array in arrays:
        value = array[(0,) * array.ndim].astype(F32)
        total = total + jnp.minimum(jnp.abs(jnp.clip(value, -1, 1).astype(jnp.int32)), 0)
    return total


def ring_rest(block, one, three):
    left, right = ring_second(one, three)
    opposite = jnp.concatenate([exchange(right, "col", 3), exchange(left, "col", 1)])
    return [block, one, opposite, three]


def pick(array, index):
    return lax.dynamic_index_in_dim(array, index, 0, keepdims=False)


def pair(flag, first, second):
    return jnp.where(flag, jnp.concatenate([second, first]), jnp.concatenate([first, second]))


def dot(left, right, dims):
    return lax.dot_general(left, right, (dims, ((), ())), preferred_element_type=F32)


def halved(term, row):
    side, high = row & 1, row >> 1
    sent = jnp.stack([term(1 - side).astype(BF16), term(3 - side).astype(BF16)])
    came = exchange(sent, "row", 1).astype(F32)
    low_sum, high_sum = term(side) + came[0], term(side + 2) + came[1]
    passed = jnp.where(high == 1, low_sum, high_sum).astype(BF16)
    return jnp.where(high == 1, high_sum, low_sum) + exchange(passed, "row", 2).astype(F32)


def turned_rows(four, row):
    side, high = row & 1, row >> 1
    halves = four.reshape(2, 2, *four.shape[1:])
    mine, came = pick(halves, high), exchange(pick(halves, 1 - high), "row", 2)
    far = pair(high == 1, mine[None], came[None])
    kept = lax.dynamic_index_in_dim(far, side, 1, keepdims=False)
    near = exchange(lax.dynamic_index_in_dim(far, 1 - side, 1, keepdims=False), "row", 1)
    both = jnp.where(side == 1, jnp.stack([near, kept], 1), jnp.stack([kept, near], 1))
    return both.reshape(4, *four.shape[1:])


def expand(pattern, size):
    return jnp.repeat(jnp.repeat(pattern, size, axis=1), size, axis=2).astype(BF16)


def shards(
    root_inverse,
    parent_link,
    parent_pivot,
    child_link_parent,
    child_link_root,
    child_pivot,
    link_pattern,
):
    leaf, row, col = (lax.axis_index(name) for name in ("leaf", "row", "col"))
    core = leaf & 1
    odd_core = core == 1
    odd_chip = (leaf & 2) == 2
    b = root_inverse.shape[-1]
    w = parent_link.shape[-1]

    def kept(array, late=0):
        return pick(array, core + late)

    def given(array, late=0):
        return pick(array, 1 - core + late)

    factors = jnp.stack([child_link_parent[:, 0], child_link_root[:, 0]], 1)
    factors = factors * expand(link_pattern[0], b // link_pattern.shape[2])[None]
    own = kept(factors)
    own_whole = lax.all_gather(own, "row")
    guest = exchange(given(factors), "leaf", 1)
    root = kept(root_inverse)
    root_one, root_three = ring_first(root, "col")

    small = jnp.stack([parent_link, parent_pivot], 1).swapaxes(2, 3)
    small_here, small_gift = kept(small), given(small)
    small_there = exchange(small_gift, "leaf", 1)
    link_two = pair(odd_core, small_here[0], small_there[0])
    link_far = pair(
        odd_core, exchange(small_here[0], "leaf", 2), exchange(small_gift[0], "leaf", 3)
    )
    link_four = pair(odd_chip, link_two, link_far)

    column = in_order(fetched(small[:, 0], "row"), row)
    column = jnp.concatenate(column, 2)
    down = pair(odd_core, kept(column), exchange(given(column), "leaf", 1))
    left, right = ring_second(root_one, root_three)
    came_one = exchange(jnp.concatenate([left, link_four]), "col", 1)
    came_three = exchange(jnp.concatenate([right, link_four]), "col", 3)
    half = b // 2
    root_two = jnp.concatenate([came_three[:half], came_one[:half]])
    root_rows = jnp.concatenate(in_order([root, root_one, root_two, root_three], col), 1)
    root_parent = (-dot(down, root_rows, ((1,), (1,)))).astype(BF16)
    links = ring_rest(link_four, came_one[half:], came_three[half:])
    far_off = row + after(links[2]) < 0
    bulk = jnp.where(far_off, jnp.stack([guest, own]), jnp.stack([own, guest]))
    bulk_one, bulk_three = ring_first(bulk, "col")
    links = [p.reshape(4, w, b) for p in links]
    links = jnp.stack(in_order(links, col), 1).reshape(4, 4 * w, b)
    total = halved(lambda m: dot(root_parent, pick(links, m), ((1,), (1,))), row)
    pivot_two = pair(core + after(bulk_one, bulk_three) == 1, small_here[1], small_there[1])
    parent_self = (pivot_two.astype(F32) - total).astype(BF16)
    pivots = child_pivot[:, 0]
    own_pivot, guest_pivot = kept(pivots), exchange(given(pivots), "leaf", 1)

    cross = pair(odd_chip, root_parent, exchange(root_parent, "leaf", 2)).reshape(4, w, b)
    turned = turned_rows(cross, row)
    guest_whole = lax.all_gather(guest, "row")
    ready = ((leaf + after(own_whole)) & 2) == 2
    parents = pair(ready, parent_self, exchange(parent_self, "leaf", 2)).reshape(4, w, b)
    across = jnp.concatenate([cross, turned, parents])
    across_one, across_three = ring_first(across, "col")
    across = ring_rest(across, across_one, across_three)
    bulk = ring_rest(bulk, bulk_one, bulk_three)
    cross = jnp.stack(in_order([p[:4] for p in across], col), 1).reshape(16 * w, b)
    turned = jnp.stack(in_order([p[4:8] for p in across], col))
    turned = turned.transpose(0, 2, 1, 3).reshape(4 * w, 4 * b)
    parents = jnp.stack(in_order([p[8:] for p in across], col), 1).reshape(16 * w, b)

    def child(whole, rows, pivot, late):
        upper = lax.dynamic_index_in_dim(whole, late, 1).reshape(4 * b, b)
        lower = lax.dynamic_index_in_dim(whole, 1 + late, 1).reshape(4 * b, b)
        child_parent = -(dot(parents, upper, ((0,), (0,))) + dot(turned, lower, ((1,), (0,))))
        child_root = -(dot(cross, upper, ((0,), (0,))) + dot(root_rows, lower, ((1,), (0,))))
        child_parent, child_root = child_parent.astype(BF16), child_root.astype(BF16)

        def term(m):
            mine = pick(rows, m)
            return dot(mine[0], child_parent, ((0,), (0,))) + dot(mine[1], child_root, ((0,), (0,)))

        total = halved(term, row)
        return jnp.stack([child_parent, child_root]), (pivot.astype(F32) - total).astype(BF16)

    rows = [jnp.stack(in_order([p[i] for p in bulk], col)) for i in range(2)]
    own_pair, own_self = child(own_whole, rows[0], own_pivot, 0)
    guest_pair, guest_self = child(guest_whole, rows[1], guest_pivot, after(own_pair))
    guest_pair, guest_self = exchange(guest_pair, "leaf", 1), exchange(guest_self, "leaf", 1)

    both = jnp.stack([root_parent, parent_self]).reshape(2, 2, w, b)
    both_there = exchange(jnp.where(odd_core, both[:, 0], both[:, 1]), "leaf", 1)
    both_here = jnp.where(odd_core, both[:, 1], both[:, 0])
    both = pair(odd_core, both_here[None], both_there[None]).swapaxes(2, 3)
    pairs = pair(odd_core, own_pair[None], guest_pair[None])
    selfs = pair(odd_core, own_self[None], guest_self[None])
    return (both[:, 0], both[:, 1], pairs[:, 0][:, None], pairs[:, 1][:, None], selfs[:, None])


def solution(mesh):
    in_specs = (
        P(None, "row", "col"),
        P(None, "row", ("leaf", "col")),
        P(None, "row", ("leaf", "col")),
        P(None, "leaf", "row", "col"),
        P(None, "leaf", "row", "col"),
        P(None, "leaf", "row", "col"),
        P("leaf", None, "row", "col"),
    )
    out_specs = (
        P(None, "row", ("leaf", "col")),
        P(None, "row", ("leaf", "col")),
        P(None, "leaf", "row", "col"),
        P(None, "leaf", "row", "col"),
        P(None, "leaf", "row", "col"),
    )
    return jax.shard_map(shards, mesh=mesh, in_specs=in_specs, out_specs=out_specs, check_vma=False)
```

```python
import jax
import jax.numpy as jnp
from jax import lax
from jax.sharding import PartitionSpec as P

BF16 = jnp.bfloat16
F32 = jnp.float32


def exchange(block, axis, bits):
    count = lax.axis_size(axis)
    return lax.ppermute(block, axis, [(i, i ^ bits) for i in range(count)])


def in_order(pieces, index):
    odd = (index & 1) == 1
    high = (index & 2) == 2
    a, b, c, d = pieces
    a, b = jnp.where(odd, b, a), jnp.where(odd, a, b)
    c, d = jnp.where(odd, d, c), jnp.where(odd, c, d)
    return [
        jnp.where(high, c, a),
        jnp.where(high, d, b),
        jnp.where(high, a, c),
        jnp.where(high, b, d),
    ]


def ring_first(block, axis):
    return exchange(block, axis, 1), exchange(block, axis, 3)


def ring_second(one, three):
    half = one.shape[0] // 2
    return three[half:], one[:half]


def after(*arrays):
    total = jnp.int32(0)
    for array in arrays:
        value = array[(0,) * array.ndim].astype(F32)
        total = total + jnp.minimum(jnp.abs(jnp.clip(value, -1, 1).astype(jnp.int32)), 0)
    return total


def ring_rest(block, one, three):
    left, right = ring_second(one, three)
    opposite = jnp.concatenate([exchange(right, "col", 3), exchange(left, "col", 1)])
    return [block, one, opposite, three]


def pick(array, index):
    return lax.dynamic_index_in_dim(array, index, 0, keepdims=False)


def pair(flag, first, second):
    return jnp.where(flag, jnp.concatenate([second, first]), jnp.concatenate([first, second]))


def dot(left, right, dims):
    return lax.dot_general(left, right, (dims, ((), ())), preferred_element_type=F32)


def doubled(block, row):
    far = pair(row >= 2, block[None], exchange(block, "row", 2)[None])
    near = exchange(far, "row", 1)
    odd = (row & 1) == 1
    first, second = jnp.where(odd, near, far), jnp.where(odd, far, near)
    return [first[0], second[0], first[1], second[1]]


def halved(term, row):
    side, high = row & 1, row >> 1
    sent = jnp.stack([term(1 - side).astype(BF16), term(3 - side).astype(BF16)])
    came = exchange(sent, "row", 1).astype(F32)
    low_sum, high_sum = term(side) + came[0], term(side + 2) + came[1]
    passed = jnp.where(high == 1, low_sum, high_sum).astype(BF16)
    return jnp.where(high == 1, high_sum, low_sum) + exchange(passed, "row", 2).astype(F32)


def turned_rows(four, row):
    side, high = row & 1, row >> 1
    halves = four.reshape(2, 2, *four.shape[1:])
    mine, came = pick(halves, high), exchange(pick(halves, 1 - high), "row", 2)
    far = pair(high == 1, mine[None], came[None])
    kept = lax.dynamic_index_in_dim(far, side, 1, keepdims=False)
    near = exchange(lax.dynamic_index_in_dim(far, 1 - side, 1, keepdims=False), "row", 1)
    both = jnp.where(side == 1, jnp.stack([near, kept], 1), jnp.stack([kept, near], 1))
    return both.reshape(4, *four.shape[1:])


def expand(pattern, size):
    return jnp.repeat(jnp.repeat(pattern, size, axis=1), size, axis=2).astype(BF16)


def shards(
    root_inverse,
    parent_link,
    parent_pivot,
    child_link_parent,
    child_link_root,
    child_pivot,
    link_pattern,
):
    leaf, row, col = (lax.axis_index(name) for name in ("leaf", "row", "col"))
    core = leaf & 1
    odd_core = core == 1
    odd_chip = (leaf & 2) == 2
    b = root_inverse.shape[-1]
    w = parent_link.shape[-1]

    def kept(array, late=0):
        return pick(array, core + late)

    def given(array, late=0):
        return pick(array, 1 - core + late)

    factors = jnp.stack([child_link_parent[:, 0], child_link_root[:, 0]], 1)
    factors = factors * expand(link_pattern[0], b // link_pattern.shape[2])[None]
    own = kept(factors)
    own_whole = lax.all_gather(own, "row")
    guest = exchange(given(factors), "leaf", 1)
    root = kept(root_inverse)
    root_one, root_three = ring_first(root, "col")

    small = jnp.stack([parent_link, parent_pivot], 1).swapaxes(2, 3)
    small_here, small_gift = kept(small), given(small)
    small_there = exchange(small_gift, "leaf", 1)
    link_two = pair(odd_core, small_here[0], small_there[0])
    link_far = pair(
        odd_core, exchange(small_here[0], "leaf", 2), exchange(small_gift[0], "leaf", 3)
    )
    link_four = pair(odd_chip, link_two, link_far)

    column = jnp.concatenate(doubled(small[:, 0], row), 2)
    down = pair(odd_core, kept(column), exchange(given(column), "leaf", 1))
    left, right = ring_second(root_one, root_three)
    came_one = exchange(jnp.concatenate([left, link_four]), "col", 1)
    came_three = exchange(jnp.concatenate([right, link_four]), "col", 3)
    half = b // 2
    root_two = jnp.concatenate([came_three[:half], came_one[:half]])
    root_rows = jnp.concatenate(in_order([root, root_one, root_two, root_three], col), 1)
    root_parent = (-dot(down, root_rows, ((1,), (1,)))).astype(BF16)
    links = ring_rest(link_four, came_one[half:], came_three[half:])
    far_off = row + after(links[2]) < 0
    bulk = jnp.where(far_off, jnp.stack([guest, own]), jnp.stack([own, guest]))
    bulk_one, bulk_three = ring_first(bulk, "col")
    links = [p.reshape(4, w, b) for p in links]
    links = jnp.stack(in_order(links, col), 1).reshape(4, 4 * w, b)
    total = halved(lambda m: dot(root_parent, pick(links, m), ((1,), (1,))), row)
    pivot_two = pair(core + after(bulk_one, bulk_three) == 1, small_here[1], small_there[1])
    parent_self = (pivot_two.astype(F32) - total).astype(BF16)
    pivots = child_pivot[:, 0]
    own_pivot, guest_pivot = kept(pivots), exchange(given(pivots), "leaf", 1)

    cross = pair(odd_chip, root_parent, exchange(root_parent, "leaf", 2)).reshape(4, w, b)
    turned = turned_rows(cross, row)
    guest_whole = lax.all_gather(guest, "row")
    ready = ((leaf + after(own_whole)) & 2) == 2
    parents = pair(ready, parent_self, exchange(parent_self, "leaf", 2)).reshape(4, w, b)
    across = jnp.concatenate([cross, turned, parents])
    across_one, across_three = ring_first(across, "col")
    across = ring_rest(across, across_one, across_three)
    bulk = ring_rest(bulk, bulk_one, bulk_three)
    cross = jnp.stack(in_order([p[:4] for p in across], col), 1).reshape(16 * w, b)
    turned = jnp.stack(in_order([p[4:8] for p in across], col))
    turned = turned.transpose(0, 2, 1, 3).reshape(4 * w, 4 * b)
    parents = jnp.stack(in_order([p[8:] for p in across], col), 1).reshape(16 * w, b)

    def child(whole, rows, pivot, late):
        upper = lax.dynamic_index_in_dim(whole, late, 1).reshape(4 * b, b)
        lower = lax.dynamic_index_in_dim(whole, 1 + late, 1).reshape(4 * b, b)
        child_parent = -(dot(parents, upper, ((0,), (0,))) + dot(turned, lower, ((1,), (0,))))
        child_root = -(dot(cross, upper, ((0,), (0,))) + dot(root_rows, lower, ((1,), (0,))))
        child_parent, child_root = child_parent.astype(BF16), child_root.astype(BF16)

        def term(m):
            mine = pick(rows, m)
            return dot(mine[0], child_parent, ((0,), (0,))) + dot(mine[1], child_root, ((0,), (0,)))

        total = halved(term, row)
        return jnp.stack([child_parent, child_root]), (pivot.astype(F32) - total).astype(BF16)

    rows = [jnp.stack(in_order([p[i] for p in bulk], col)) for i in range(2)]
    own_pair, own_self = child(own_whole, rows[0], own_pivot, 0)
    guest_pair, guest_self = child(guest_whole, rows[1], guest_pivot, after(own_pair))
    guest_pair, guest_self = exchange(guest_pair, "leaf", 1), exchange(guest_self, "leaf", 1)

    both = jnp.stack([root_parent, parent_self]).reshape(2, 2, w, b)
    both_there = exchange(jnp.where(odd_core, both[:, 0], both[:, 1]), "leaf", 1)
    both_here = jnp.where(odd_core, both[:, 1], both[:, 0])
    both = pair(odd_core, both_here[None], both_there[None]).swapaxes(2, 3)
    pairs = pair(odd_core, own_pair[None], guest_pair[None])
    selfs = pair(odd_core, own_self[None], guest_self[None])
    return (both[:, 0], both[:, 1], pairs[:, 0][:, None], pairs[:, 1][:, None], selfs[:, None])


def solution(mesh):
    in_specs = (
        P(None, "row", "col"),
        P(None, "row", ("leaf", "col")),
        P(None, "row", ("leaf", "col")),
        P(None, "leaf", "row", "col"),
        P(None, "leaf", "row", "col"),
        P(None, "leaf", "row", "col"),
        P("leaf", None, "row", "col"),
    )
    out_specs = (
        P(None, "row", ("leaf", "col")),
        P(None, "row", ("leaf", "col")),
        P(None, "leaf", "row", "col"),
        P(None, "leaf", "row", "col"),
        P(None, "leaf", "row", "col"),
    )
    return jax.shard_map(shards, mesh=mesh, in_specs=in_specs, out_specs=out_specs, check_vma=False)
```
